32 devices in a mesh: dp: 16 (over z, y, core), node: 2 (over x).
Axes of the slice: x: 2, y: 2, z: 4, core: 2. Of those that a mesh axis runs over, the one named last changes fastest.
Arguments:
- tokens: bfloat16 [256, 4096], P('dp', 'node'), may hold values from -200 to 200
- cotangent: bfloat16 [256, 4096], P('dp', 'node'), may hold values from -6 to 6
- norm_gain: float32 [4096], P('node'), may hold values from 0.1 to 1.9
- gate_weight: bfloat16 [10240, 4096], P('dp', 'node'), may hold values from -0.09375 to 0.09375
- up_weight: bfloat16 [10240, 4096], P('dp', 'node'), may hold values from -0.09375 to 0.09375
- down_weight: bfloat16 [10240, 4096], P('dp', 'node'), may hold values from -0.0625 to 0.0625
Outputs:
- branch_out: bfloat16 [256, 4096], P('dp', 'node')
- grad_tokens: bfloat16 [256, 4096], P('dp', 'node')
- grad_gate_weight: float32 [10240, 4096], P('dp', 'node')
- grad_up_weight: float32 [10240, 4096], P('dp', 'node')
- grad_down_weight: float32 [10240, 4096], P('dp', 'node')
- grad_norm_gain: float32 [4096], P('node')
The draws below stay inside these ranges and needn't reach their ends.
All inputs are finite; a program needn't handle non-finite values.
Results may differ from the reference program's by a relative error of at most 0.0065.
Values may be sent and summed in bfloat16 or wider, within the bound.
No kernel may reach another device: no remote copies, remote signals or barrier semaphores. Data moves between devices by JAX's collectives and lax.ppermute only.
A program may use at most 64 MiB of HBM per device.

```python
import math
import jax
import jax.numpy as jnp
from jax import lax

D = 4096
FF = 10240
TOK = 256


def draw_tokens(key, part):
    key = jax.random.fold_in(key, 11)
    first, second, third = jax.random.split(key, 3)
    position = jnp.arange(D, dtype=jnp.float32) / (D - 1)
    base = jnp.clip(jax.random.normal(first, (TOK, D), jnp.float32), -6.0, 6.0)
    column_power = 0.5 * position + 0.5 * jax.random.uniform(second, (D,), jnp.float32)
    row_power = 0.5 * jax.random.uniform(third, (TOK, 1), jnp.float32, -1.0, 1.0)
    values = base * jnp.power(10.0, column_power)[None, :] * jnp.power(10.0, row_power)
    return values.astype(jnp.bfloat16)


def block_scale(rng, shape, shards, smallest, top_value):
    gain = 1.0
    for dim, parts in shards:
        steps = jax.random.uniform(jax.random.fold_in(jax.random.fold_in(rng, 6), dim), (parts,), jnp.float32, smallest / len(shards), top_value / len(shards))
        gain = gain * jnp.repeat(jnp.exp(steps), shape[dim] // parts).reshape((-1,) + (1,) * (len(shape) - 1 - dim))
    return gain


def noise(key, dims, deviation, reach, cuts=(), kind=jnp.bfloat16):
    result = deviation * jax.random.normal(key, dims, jnp.float32)
    if cuts:
        result = result * block_scale(key, dims, cuts, -0.22, 0.18)
    return jnp.clip(result, -reach, reach).astype(kind)


def setup_inputs(seed: int = 0) -> dict:
    keys = jax.random.split(jax.random.key(seed), 7)
    return {
        "tokens": draw_tokens(jax.random.fold_in(keys[6], 71), 0),
        "cotangent": noise(keys[1], (TOK, D), 1.0, 6.0, ((0, 16), (1, 2))),
        "norm_gain": jnp.clip(1.0 + 0.18 * jax.random.normal(keys[2], (D,), jnp.float32), 0.1, 1.9),
        "gate_weight": noise(keys[3], (FF, D), D ** -0.5, 0.09375, ((0, 16), (1, 2))),
        "up_weight": noise(keys[4], (FF, D), D ** -0.5, 0.09375, ((0, 16), (1, 2))),
        "down_weight": noise(keys[5], (FF, D), FF ** -0.5, 0.0625, ((0, 16), (1, 2))),
    }


EPSILON = 1e-06
GELU_SCALE = math.sqrt(2.0 / math.pi)

def gelu_parts(value):
    inner = GELU_SCALE * (value + 0.044715 * value * value * value)
    tanh_inner = jnp.tanh(inner)
    activated = 0.5 * value * (1.0 + tanh_inner)
    slope = 0.5 * (1.0 + tanh_inner) + 0.5 * value * (1.0 - tanh_inner * tanh_inner) * GELU_SCALE * (1.0 + 3.0 * 0.044715 * value * value)
    return (activated, slope)

def reference(tokens, cotangent, norm_gain, gate_weight, up_weight, down_weight):
    widened = tokens.astype(jnp.float32)
    mean_square = lax.optimization_barrier(jnp.mean(widened * widened, axis=1))
    inv_rms = lax.rsqrt(mean_square + EPSILON)
    scaled = widened * inv_rms[:, None]
    normed = (scaled * norm_gain).astype(jnp.bfloat16)
    gate_value = jnp.dot(gate_weight, normed.T, preferred_element_type=jnp.float32)
    up_value = jnp.dot(up_weight, normed.T, preferred_element_type=jnp.float32)
    activated, slope = gelu_parts(gate_value)
    hidden = (activated * up_value).astype(jnp.bfloat16)
    branch_out = jnp.dot(hidden.T, down_weight, preferred_element_type=jnp.float32).astype(jnp.bfloat16)
    back_hidden = jnp.dot(down_weight, cotangent.T, preferred_element_type=jnp.float32)
    grad_gate = (back_hidden * up_value * slope).astype(jnp.bfloat16)
    grad_up = (back_hidden * activated).astype(jnp.bfloat16)
    grad_down_weight = jnp.dot(hidden, cotangent, preferred_element_type=jnp.float32)
    grad_gate_weight = jnp.dot(grad_gate, normed, preferred_element_type=jnp.float32)
    grad_up_weight = jnp.dot(grad_up, normed, preferred_element_type=jnp.float32)
    grad_normed = jnp.dot(grad_gate.T, gate_weight, preferred_element_type=jnp.float32) + jnp.dot(grad_up.T, up_weight, preferred_element_type=jnp.float32)
    grad_norm_gain = lax.optimization_barrier(jnp.sum(grad_normed * scaled, axis=0))
    grad_scaled = grad_normed * norm_gain
    row_mean = lax.optimization_barrier(jnp.mean(grad_scaled * scaled, axis=1))
    grad_tokens = (inv_rms[:, None] * (grad_scaled - scaled * row_mean[:, None])).astype(jnp.bfloat16)
    return (branch_out, grad_tokens, grad_gate_weight, grad_up_weight, grad_down_weight, grad_norm_gain)
```

```python
import functools
import math

import jax
import jax.numpy as jnp
from jax import lax
from jax.experimental import pallas as pl
from jax.experimental.pallas import tpu as pltpu
from jax.sharding import PartitionSpec as P

EPSILON = 1e-06
GELU_SCALE = math.sqrt(2.0 / math.pi)
BF16 = jnp.bfloat16
F32 = jnp.float32


def gelu_parts(value):
    inner = GELU_SCALE * (value + 0.044715 * value * value * value)
    tanh_inner = jnp.tanh(inner)
    activated = 0.5 * value * (1.0 + tanh_inner)
    slope = 0.5 * (1.0 + tanh_inner) + 0.5 * value * (
        1.0 - tanh_inner * tanh_inner
    ) * GELU_SCALE * (1.0 + 3.0 * 0.044715 * value * value)
    return (activated, slope)


def swap(value, axis, size, distance):
    return lax.ppermute(value, axis, [(i, i ^ distance) for i in range(size)])


def node_sum(value, node):
    bit = 1
    while bit < node:
        value = value + swap(value.astype(BF16), "node", node, bit).astype(F32)
        bit *= 2
    return value


def halving_distances(dp):
    distances = []
    bit = 4
    while bit < dp:
        distances.append(bit)
        bit *= 2
    return distances


def direct_steps(dp):
    distances, steps = halving_distances(dp), []
    while distances:
        low, *high = distances[:2]
        steps.append([high[0], low, low ^ high[0]] if high else [low])
        distances = distances[2:]
    return steps


def gather_rows(rows, dp):
    for parts in reversed(direct_steps(dp)):
        rows = jnp.concatenate([rows] + [swap(rows, "dp", dp, d) for d in parts], axis=0)
    rows = lax.optimization_barrier(rows)
    return jnp.concatenate([rows, swap(rows, "dp", dp, 2)], axis=0), rows


def gather_rows_behind(rows, dp, behind, used_behind):
    for place, distance in enumerate(reversed(halving_distances(dp))):
        if place == 1:
            rows = after(rows, behind)
        rows = jnp.concatenate([rows, swap(rows, "dp", dp, distance)], axis=0)
    return jnp.concatenate([rows, after(swap(rows, "dp", dp, 2), used_behind)], axis=0)


def inward(rows, weight):
    return lax.dot_general(rows, weight, (((1,), (1,)), ((), ())), preferred_element_type=F32)


def outward(rows, weight):
    return lax.dot_general(rows, weight, (((1,), (0,)), ((), ())), preferred_element_type=F32)


def grad_kernel(count, *refs):
    rows, inputs = refs[: 2 * count], refs[2 * count : 2 * count + 2]
    outs, (mark, turned) = refs[-count - 2 : -2], refs[-2:]
    half, units = rows[0].shape

    @pl.when(pl.program_id(0) == 0)
    def _():
        mark[...] = jnp.zeros(mark.shape, F32)
        for place, ref in enumerate(rows):
            piece, k = divmod(place, count)
            turned[k * units : (k + 1) * units, piece * half : (piece + 1) * half] = ref[...].T

    block = jnp.concatenate([ref[...] for ref in inputs], axis=0)
    for k in range(count):
        outs[k][...] = jnp.dot(
            turned[k * units : (k + 1) * units, :], block, preferred_element_type=F32
        )


def weight_grads(count, rows, inputs, behind):
    units, width = rows[0].shape[1], inputs[0].shape[1]
    block = min(width, 512)
    whole = lambda a: pl.BlockSpec(a.shape, lambda i: (0, 0))
    columns = lambda a: pl.BlockSpec((a.shape[0], block), lambda i: (0, i))
    return pl.pallas_call(
        functools.partial(grad_kernel, count),
        grid=(width // block,),
        in_specs=[whole(a) for a in rows]
        + [columns(a) for a in inputs]
        + [pl.BlockSpec(memory_space=pl.ANY)] * len(behind),
        out_specs=[pl.BlockSpec((units, block), lambda i: (0, i))] * count
        + [pl.BlockSpec((8, width), lambda i: (0, 0))],
        out_shape=[jax.ShapeDtypeStruct((units, width), F32)] * count
        + [jax.ShapeDtypeStruct((8, width), F32)],
        scratch_shapes=[pltpu.VMEM((count * units, 2 * rows[0].shape[0]), BF16)],
        compiler_params=pltpu.CompilerParams(vmem_limit_bytes=20 * 2**20),
        cost_estimate=pl.CostEstimate(flops=1000, bytes_accessed=1000, transcendentals=0),
        name="weight_grads",
    )(*rows, *inputs, *behind)


def add_kernel(kept_ref, got_ref, *refs):
    refs[-1][...] = kept_ref[...] + got_ref[...].astype(F32)


def add_got(kept, got, bytes_accessed, behind=()):
    return pl.pallas_call(
        add_kernel,
        in_specs=[pl.BlockSpec(memory_space=pltpu.VMEM)] * 2
        + [pl.BlockSpec(memory_space=pl.ANY)] * len(behind),
        out_shape=jax.ShapeDtypeStruct(kept.shape, F32),
        compiler_params=pltpu.CompilerParams(vmem_limit_bytes=8 * 2**20),
        cost_estimate=pl.CostEstimate(flops=1, bytes_accessed=bytes_accessed, transcendentals=0),
        name="add_got",
    )(kept, got, *behind)


def gain_kernel(*refs):
    products, inputs, gain, out = refs[:3], refs[3:5], refs[5], refs[6]
    half = products[0].shape[0]
    rows = [inputs[0][:half], inputs[0][half:], inputs[1][...]]
    total = jnp.zeros(out.shape, F32)
    for product, tokens in zip(products, rows):
        terms = product[...].astype(F32) * tokens.astype(F32)
        total = total + jnp.sum(terms, axis=0, keepdims=True)
    out[...] = total / gain[...]


def gain_sums(products, inputs, gain):
    out = pl.pallas_call(
        gain_kernel,
        out_shape=jax.ShapeDtypeStruct((1, gain.shape[0]), F32),
        compiler_params=pltpu.CompilerParams(vmem_limit_bytes=8 * 2**20),
        cost_estimate=pl.CostEstimate(flops=1000, bytes_accessed=1000, transcendentals=0),
        name="gain_sums",
    )(*products, *inputs, gain[None, :])
    return out


def after(value, dep):
    width = value.shape[1]
    if dep.shape[1] >= width:
        row = lax.slice(dep, (0, 0), (1, width))
    else:
        row = lax.slice(dep, (0, 0), (1, math.gcd(dep.shape[1], width)))
        row = jnp.tile(row, (1, width // row.shape[1]))
    return jnp.where(row == row, value, jnp.zeros_like(value))


def on_device(dp, node, tokens, cotangent, norm_gain, gate_weight, up_weight, down_weight):
    features = tokens.shape[1] * node
    widened = tokens.astype(F32)
    square_sum = jnp.sum(widened * widened, axis=1)
    bit = 1
    while bit < node:
        square_sum = square_sum + swap(square_sum, "node", node, bit)
        bit *= 2
    inv_rms = lax.rsqrt(square_sum / features + EPSILON)[:, None]
    scaled = widened * inv_rms
    normed_rows = (scaled * norm_gain).astype(BF16)
    own_n, sent_n = gather_rows(normed_rows, dp)
    size = own_n.shape[0] // 2
    other_n = swap(own_n, "dp", dp, 1)

    def project(rows):
        return jnp.concatenate([inward(rows, gate_weight), inward(rows, up_weight)], axis=0)

    own_p = project(own_n)
    own_c = gather_rows_behind(cotangent, dp, sent_n, own_p)
    other_c = swap(own_c, "dp", dp, 1)
    other_p = project(other_n)
    other_b = after(inward(other_c, down_weight), other_p)
    own_b = after(inward(own_c, down_weight), other_b)
    own_p = after(node_sum(own_p, node), own_b)
    other_p, other_b = node_sum(other_p, node), node_sum(other_b, node)
    own_b = node_sum(own_b, node)

    def activate(both):
        gate_value, up_value = both[: 2 * size], both[2 * size :]
        activated, slope = gelu_parts(gate_value)
        hidden = (activated * up_value).astype(BF16)
        lean = slope * up_value
        row_factor = lean * gate_value + activated * up_value
        return lax.optimization_barrier((hidden, activated, lean, row_factor))

    def grads(back, activated, lean, row_factor):
        grad_gate, grad_up = (back * lean).astype(BF16), (back * activated).astype(BF16)
        row_part = jnp.sum(back * row_factor, axis=1)[None, :]
        return lax.optimization_barrier(((grad_gate, grad_up), row_part))

    def outward_pair(pair):
        return outward(pair[0], gate_weight) + outward(pair[1], up_weight)

    own_h, *own_f = activate(own_p)
    other_h, *other_f = activate(other_p)
    sent_h = outward(other_h, down_weight).astype(BF16)
    got_h = swap(sent_h, "dp", dp, 1)
    branch_sent = outward(own_h[size:], down_weight) + got_h[size:].astype(F32)
    branch_sent = lax.optimization_barrier(branch_sent.astype(BF16))
    branch = outward(own_h[:size], down_weight) + got_h[:size].astype(F32)
    grad_down_weight, mark = weight_grads(1, (own_h, other_h), (own_c, other_c), (sent_h,))

    other_g, other_r = grads(after(other_b, mark), *other_f)
    sent_g = outward_pair(other_g).astype(BF16)
    got_g = swap(sent_g, "dp", dp, 1)
    own_b = after(after(own_b, branch_sent), sent_g)
    own_g, own_r = grads(own_b, *own_f)
    normed_y = outward_pair([rows[size:] for rows in own_g])
    normed_sent = lax.optimization_barrier((normed_y + got_g[size:].astype(F32)).astype(BF16))
    normed_own = outward_pair([after(rows[:size], normed_sent) for rows in own_g])
    gain_part = gain_sums((normed_own, normed_y, sent_g), (own_n, other_n), norm_gain)
    width = gain_part.shape[1]

    def vector(distance, gain, rows):
        return swap(jnp.concatenate([gain, rows], axis=1), "dp", dp, distance)

    got_v = [
        vector(1, gain_part, other_r[:, :size]),
        vector(2, gain_part, own_r[:, size:]),
        vector(3, gain_part, other_r[:, size:]),
    ]
    branch = add_got(branch, swap(branch_sent, "dp", dp, 2), 40_000_000, (gain_part,))
    distances = halving_distances(dp)
    half = branch.shape[0] // 2
    sent_h = lax.optimization_barrier(branch[half:].astype(BF16))
    grad_gate_weight, grad_up_weight, mark = weight_grads(
        2, (*own_g, *other_g), (own_n, other_n), (gain_part, sent_h)
    )
    for distance in distances[1:]:
        branch = branch[:half] + swap(sent_h, "dp", dp, distances[0]).astype(F32)
        distances, half = distances[1:], half // 2
        sent_h = lax.optimization_barrier(branch[half:].astype(BF16))
    branch = branch[:half] + swap(sent_h, "dp", dp, distances[0]).astype(F32)

    normed = normed_own + got_g[:size].astype(F32)
    normed = add_got(normed, swap(normed_sent, "dp", dp, 2), 40_000_000, (mark,))
    normed = after(normed, sent_h)
    vectors = jnp.concatenate([after(gain_part, mark), own_r[:, :size]], axis=1)
    vectors = vectors + (got_v[0] + got_v[1] + got_v[2])
    gain_part, rows = after(vectors[:, :width], normed), after(vectors[:, width:], normed)
    for parts in direct_steps(dp):
        count = normed.shape[0] // (len(parts) + 1)
        extra = gain_part.reshape(count, -1)
        lanes = extra.shape[1]
        joined = [
            jnp.concatenate(
                [normed[place * count : (place + 1) * count], extra]
                + [jnp.pad(rows[:, place * count : (place + 1) * count], ((0, count - 1), (0, 0)))],
                axis=1,
            )
            for place in range(len(parts) + 1)
        ]
        total = joined[0]
        for place, distance in enumerate(parts):
            sent = joined[place + 1].astype(BF16)
            total = total + swap(sent, "dp", dp, distance).astype(F32)
        normed = total[:, :width]
        gain_part = total[:, width : width + lanes].reshape(1, width)
        rows = total[:1, width + lanes :]

    row_mean = (rows / features).reshape(-1, 1)
    grad_scaled = normed * norm_gain
    grad_tokens = (inv_rms * (grad_scaled - scaled * row_mean)).astype(BF16)
    return (
        branch.astype(BF16),
        grad_tokens,
        grad_gate_weight,
        grad_up_weight,
        grad_down_weight,
        gain_part[0],
    )


def solution(mesh):
    dp, node = mesh.shape["dp"], mesh.shape["node"]

    def run(*arrays):
        return on_device(dp, node, *arrays)

    grid = P("dp", "node")
    return jax.shard_map(
        run,
        mesh=mesh,
        in_specs=(grid, grid, P("node"), grid, grid, grid),
        out_specs=(grid, grid, grid, grid, grid, P("node")),
        check_vma=False,
    )
```

```python
import functools
import math

import jax
import jax.numpy as jnp
from jax import lax
from jax.experimental import pallas as pl
from jax.experimental.pallas import tpu as pltpu
from jax.sharding import PartitionSpec as P

EPSILON = 1e-06
GELU_SCALE = math.sqrt(2.0 / math.pi)
BF16 = jnp.bfloat16
F32 = jnp.float32


def gelu_parts(value):
    inner = GELU_SCALE * (value + 0.044715 * value * value * value)
    tanh_inner = jnp.tanh(inner)
    activated = 0.5 * value * (1.0 + tanh_inner)
    slope = 0.5 * (1.0 + tanh_inner) + 0.5 * value * (
        1.0 - tanh_inner * tanh_inner
    ) * GELU_SCALE * (1.0 + 3.0 * 0.044715 * value * value)
    return (activated, slope)


def swap(value, axis, size, distance):
    return lax.ppermute(value, axis, [(i, i ^ distance) for i in range(size)])


def node_sum(value, node):
    bit = 1
    while bit < node:
        value = value + swap(value.astype(BF16), "node", node, bit).astype(F32)
        bit *= 2
    return value


def halving_distances(dp):
    distances = []
    bit = 4
    while bit < dp:
        distances.append(bit)
        bit *= 2
    return distances


def direct_steps(dp):
    distances, steps = halving_distances(dp), []
    while distances:
        low, *high = distances[:2]
        steps.append([high[0], low, low ^ high[0]] if high else [low])
        distances = distances[2:]
    return steps


def gather_rows(rows, dp):
    for parts in reversed(direct_steps(dp)):
        rows = jnp.concatenate([rows] + [swap(rows, "dp", dp, d) for d in parts], axis=0)
    return jnp.concatenate([rows, swap(rows, "dp", dp, 2)], axis=0)


def gather_rows_behind(rows, dp, used_behind):
    for distance in reversed(halving_distances(dp)):
        rows = jnp.concatenate([rows, swap(rows, "dp", dp, distance)], axis=0)
    got = swap(rows, "dp", dp, 2)
    return jnp.concatenate([rows, after(got, used_behind)], axis=0)


def inward(rows, weight):
    return lax.dot_general(rows, weight, (((1,), (1,)), ((), ())), preferred_element_type=F32)


def outward(rows, weight):
    return lax.dot_general(rows, weight, (((1,), (0,)), ((), ())), preferred_element_type=F32)


def grad_kernel(count, *refs):
    rows, inputs = refs[: 2 * count], refs[2 * count : 2 * count + 2]
    outs, (mark, turned) = refs[-count - 2 : -2], refs[-2:]
    half, units = rows[0].shape

    @pl.when(pl.program_id(0) == 0)
    def _():
        mark[...] = jnp.zeros(mark.shape, F32)
        for place, ref in enumerate(rows):
            piece, k = divmod(place, count)
            turned[k * units : (k + 1) * units, piece * half : (piece + 1) * half] = ref[...].T

    block = jnp.concatenate([ref[...] for ref in inputs], axis=0)
    for k in range(count):
        outs[k][...] = jnp.dot(
            turned[k * units : (k + 1) * units, :], block, preferred_element_type=F32
        )


def weight_grads(count, rows, inputs, behind, bytes_accessed):
    units, width = rows[0].shape[1], inputs[0].shape[1]
    block = min(width, 512)
    whole = lambda a: pl.BlockSpec(a.shape, lambda i: (0, 0))
    columns = lambda a: pl.BlockSpec((a.shape[0], block), lambda i: (0, i))
    return pl.pallas_call(
        functools.partial(grad_kernel, count),
        grid=(width // block,),
        in_specs=[whole(a) for a in rows]
        + [columns(a) for a in inputs]
        + [pl.BlockSpec(memory_space=pl.ANY)] * len(behind),
        out_specs=[pl.BlockSpec((units, block), lambda i: (0, i))] * count
        + [pl.BlockSpec((8, width), lambda i: (0, 0))],
        out_shape=[jax.ShapeDtypeStruct((units, width), F32)] * count
        + [jax.ShapeDtypeStruct((8, width), F32)],
        scratch_shapes=[pltpu.VMEM((count * units, 2 * rows[0].shape[0]), BF16)],
        compiler_params=pltpu.CompilerParams(vmem_limit_bytes=20 * 2**20),
        cost_estimate=pl.CostEstimate(flops=1, bytes_accessed=bytes_accessed, transcendentals=0),
        name="weight_grads",
    )(*rows, *inputs, *behind)


def add_kernel(kept_ref, got_ref, *refs):
    refs[-1][...] = kept_ref[...] + got_ref[...].astype(F32)


def add_got(kept, got, bytes_accessed, behind=()):
    return pl.pallas_call(
        add_kernel,
        in_specs=[pl.BlockSpec(memory_space=pltpu.VMEM)] * 2
        + [pl.BlockSpec(memory_space=pl.ANY)] * len(behind),
        out_shape=jax.ShapeDtypeStruct(kept.shape, F32),
        compiler_params=pltpu.CompilerParams(vmem_limit_bytes=8 * 2**20),
        cost_estimate=pl.CostEstimate(flops=1, bytes_accessed=bytes_accessed, transcendentals=0),
        name="add_got",
    )(kept, got, *behind)


def gain_kernel(*refs):
    products, inputs, gain, out = refs[:3], refs[3:5], refs[5], refs[6]
    half = products[0].shape[0]
    rows = [inputs[0][:half], inputs[0][half:], inputs[1][...]]
    total = jnp.zeros(out.shape, F32)
    for product, tokens in zip(products, rows):
        terms = product[...].astype(F32) * tokens.astype(F32)
        total = total + jnp.sum(terms, axis=0, keepdims=True)
    out[...] = total / gain[...]


def gain_sums(products, inputs, gain):
    out = pl.pallas_call(
        gain_kernel,
        out_shape=jax.ShapeDtypeStruct((1, gain.shape[0]), F32),
        compiler_params=pltpu.CompilerParams(vmem_limit_bytes=8 * 2**20),
        cost_estimate=pl.CostEstimate(flops=1000, bytes_accessed=1000, transcendentals=0),
        name="gain_sums",
    )(*products, *inputs, gain[None, :])
    return out


def after(value, dep):
    width = value.shape[1]
    if dep.shape[1] >= width:
        row = lax.slice(dep, (0, 0), (1, width))
    else:
        row = lax.slice(dep, (0, 0), (1, math.gcd(dep.shape[1], width)))
        row = jnp.tile(row, (1, width // row.shape[1]))
    return jnp.where(row == row, value, jnp.zeros_like(value))


def on_device(dp, node, tokens, cotangent, norm_gain, gate_weight, up_weight, down_weight):
    features = tokens.shape[1] * node
    widened = tokens.astype(F32)
    square_sum = jnp.sum(widened * widened, axis=1)
    bit = 1
    while bit < node:
        square_sum = square_sum + swap(square_sum, "node", node, bit)
        bit *= 2
    inv_rms = lax.rsqrt(square_sum / features + EPSILON)[:, None]
    scaled = widened * inv_rms
    normed_rows = (scaled * norm_gain).astype(BF16)
    own_n = gather_rows(normed_rows, dp)
    size = own_n.shape[0] // 2
    other_n = swap(own_n, "dp", dp, 1)

    def project(rows):
        return jnp.concatenate([inward(rows, gate_weight), inward(rows, up_weight)], axis=0)

    own_p = project(own_n)
    other_p = project(other_n)
    own_c = gather_rows_behind(cotangent, dp, own_p[2 * size :])
    other_c = swap(own_c, "dp", dp, 1)
    other_b = after(inward(other_c, down_weight), other_p)
    own_b = after(inward(own_c, down_weight), other_b)
    own_p = after(node_sum(own_p, node), own_b)
    other_p, own_b = node_sum(other_p, node), node_sum(own_b, node)

    def activate(both):
        gate_value, up_value = both[: 2 * size], both[2 * size :]
        activated, slope = gelu_parts(gate_value)
        hidden = (activated * up_value).astype(BF16)
        lean = slope * up_value
        row_factor = lean * gate_value + activated * up_value
        return lax.optimization_barrier((hidden, activated, lean, row_factor))

    def grads(back, activated, lean, row_factor):
        grad_gate, grad_up = (back * lean).astype(BF16), (back * activated).astype(BF16)
        row_part = jnp.sum(back * row_factor, axis=1)[None, :]
        return lax.optimization_barrier(((grad_gate, grad_up), row_part))

    def outward_pair(pair):
        return outward(pair[0], gate_weight) + outward(pair[1], up_weight)

    own_h, *own_f = activate(own_p)
    other_h, *other_f = activate(other_p)
    sent_h = outward(other_h, down_weight).astype(BF16)
    got_h = swap(sent_h, "dp", dp, 1)
    branch_sent = outward(own_h[size:], down_weight) + got_h[size:].astype(F32)
    branch_sent = lax.optimization_barrier(branch_sent.astype(BF16))
    branch = outward(own_h[:size], down_weight) + got_h[:size].astype(F32)
    bit = 1
    while bit < node:
        got = swap(other_b.astype(BF16), "node", node, bit)
        other_b = add_got(other_b, got, 40_000_000, (sent_h,))
        bit *= 2
    other_g, other_r = grads(other_b, *other_f)
    sent_g = outward_pair(other_g).astype(BF16)
    got_g = swap(sent_g, "dp", dp, 1)
    own_b = after(after(own_b, branch_sent), sent_g)
    own_g, own_r = grads(own_b, *own_f)
    normed_y = outward_pair([rows[size:] for rows in own_g])
    normed_sent = lax.optimization_barrier((normed_y + got_g[size:].astype(F32)).astype(BF16))
    normed_own = outward_pair([after(rows[:size], normed_sent) for rows in own_g])
    gain_part = gain_sums((normed_own, normed_y, sent_g), (own_n, other_n), norm_gain)
    width = gain_part.shape[1]

    def vector(distance, gain, rows):
        return swap(jnp.concatenate([gain, rows], axis=1), "dp", dp, distance)

    got_v = [
        vector(1, gain_part, other_r[:, :size]),
        vector(2, gain_part, own_r[:, size:]),
        vector(3, gain_part, other_r[:, size:]),
    ]
    grad_down_weight, mark = weight_grads(
        1, (own_h, other_h), (own_c, other_c), (gain_part,), 1_000
    )
    branch = add_got(branch, swap(branch_sent, "dp", dp, 2), 40_000_000, (mark,))
    sent_h = lax.optimization_barrier(branch[branch.shape[0] // 2 :].astype(BF16))

    normed = normed_own + got_g[:size].astype(F32)
    normed = add_got(normed, swap(normed_sent, "dp", dp, 2), 40_000_000, (mark,))
    normed = after(normed, sent_h)
    vectors = jnp.concatenate([after(gain_part, normed), own_r[:, :size]], axis=1)
    vectors = vectors + (got_v[0] + got_v[1] + got_v[2])
    gain_part, rows = vectors[:, :width], vectors[:, width:]
    for parts in direct_steps(dp):
        count = normed.shape[0] // (len(parts) + 1)
        extra = gain_part.reshape(count, -1)
        lanes = extra.shape[1]

        def joined(place):
            own_rows = rows[:, place * count : (place + 1) * count]
            return [
                normed[place * count : (place + 1) * count],
                extra,
                jnp.pad(own_rows, ((0, count - 1), (0, 0))),
            ]

        sent = [jnp.concatenate(joined(k + 1), axis=1).astype(BF16) for k in range(len(parts))]
        for place, distance in enumerate(sorted(parts)[:2]):
            half = branch.shape[0] // 2
            if place:
                sent_h = after(branch[half:].astype(BF16), sent[0])
            branch = branch[:half] + swap(sent_h, "dp", dp, distance).astype(F32)
        if branch.shape[0] == count and count == tokens.shape[0]:
            grad_gate_weight, grad_up_weight, sent_h = weight_grads(
                2, (*own_g, *other_g), (own_n, other_n), (sent[-1], sent_h), 60_000_000
            )
        kept, *others = joined(0)
        total = jnp.concatenate([after(kept, sent_h), *others], axis=1)
        for part, distance in zip(sent, parts):
            total = total + swap(part, "dp", dp, distance).astype(F32)
        normed = total[:, :width]
        gain_part = total[:, width : width + lanes].reshape(1, width)
        rows = total[:1, width + lanes :]
        sent_h = branch[branch.shape[0] // 2 :].astype(BF16)

    row_mean = (rows / features).reshape(-1, 1)
    grad_scaled = normed * norm_gain
    grad_tokens = (inv_rms * (grad_scaled - scaled * row_mean)).astype(BF16)
    return (
        branch.astype(BF16),
        grad_tokens,
        grad_gate_weight,
        grad_up_weight,
        grad_down_weight,
        gain_part[0],
    )


def solution(mesh):
    dp, node = mesh.shape["dp"], mesh.shape["node"]

    def run(*arrays):
        return on_device(dp, node, *arrays)

    grid = P("dp", "node")
    return jax.shard_map(
        run,
        mesh=mesh,
        in_specs=(grid, grid, P("node"), grid, grid, grid),
        out_specs=(grid, grid, grid, grid, grid, P("node")),
        check_vma=False,
    )
```

```python
import functools
import math

import jax
import jax.numpy as jnp
from jax import lax
from jax.experimental import pallas as pl
from jax.experimental.pallas import tpu as pltpu
from jax.sharding import PartitionSpec as P

EPSILON = 1e-06
GELU_SCALE = math.sqrt(2.0 / math.pi)
BF16 = jnp.bfloat16
F32 = jnp.float32


def gelu_parts(value):
    inner = GELU_SCALE * (value + 0.044715 * value * value * value)
    tanh_inner = jnp.tanh(inner)
    activated = 0.5 * value * (1.0 + tanh_inner)
    slope = 0.5 * (1.0 + tanh_inner) + 0.5 * value * (
        1.0 - tanh_inner * tanh_inner
    ) * GELU_SCALE * (1.0 + 3.0 * 0.044715 * value * value)
    return (activated, slope)


def swap(value, axis, size, distance):
    return lax.ppermute(value, axis, [(i, i ^ distance) for i in range(size)])


def node_sum(value, node):
    bit = 1
    while bit < node:
        value = value + swap(value.astype(BF16), "node", node, bit).astype(F32)
        bit *= 2
    return value


def halving_distances(dp):
    distances = []
    bit = 4
    while bit < dp:
        distances.append(bit)
        bit *= 2
    return distances


def direct_steps(dp):
    distances, steps = halving_distances(dp), []
    while distances:
        low, *high = distances[:2]
        steps.append([high[0], low, low ^ high[0]] if high else [low])
        distances = distances[2:]
    return steps


def halve(rows):
    half, quarter = rows.shape[0] // 2, rows.shape[0] // 4
    kept = jnp.concatenate([rows[:quarter], rows[half : half + quarter]], axis=0)
    return kept, jnp.concatenate([rows[quarter:half], rows[half + quarter :]], axis=0)


def gather_rows(rows, dp):
    for parts in reversed(direct_steps(dp)):
        rows = jnp.concatenate([rows] + [swap(rows, "dp", dp, d) for d in parts], axis=0)
    return jnp.concatenate([rows, swap(rows, "dp", dp, 2)], axis=0)


def gather_rows_behind(rows, dp, used_behind):
    for distance in reversed(halving_distances(dp)):
        rows = jnp.concatenate([rows, swap(rows, "dp", dp, distance)], axis=0)
    got = swap(rows, "dp", dp, 2)
    return jnp.concatenate([rows, after(got, used_behind)], axis=0)


def inward(rows, weight):
    return lax.dot_general(rows, weight, (((1,), (1,)), ((), ())), preferred_element_type=F32)


def outward(rows, weight):
    return lax.dot_general(rows, weight, (((1,), (0,)), ((), ())), preferred_element_type=F32)


def grad_kernel(*refs):
    rows, normed, cotangent = refs[:6], refs[6:8], refs[8:10]
    outs, (mark, turned) = refs[-5:-2], refs[-2:]
    half, units = rows[0].shape

    @pl.when(pl.program_id(0) == 0)
    def _():
        mark[...] = jnp.zeros(mark.shape, F32)
        for place, ref in enumerate(rows):
            piece, k = divmod(place, 3)
            turned[k * units : (k + 1) * units, piece * half : (piece + 1) * half] = ref[...].T

    for k, inputs in enumerate((normed, normed, cotangent)):
        block = jnp.concatenate([ref[...] for ref in inputs], axis=0)
        outs[k][...] = jnp.dot(
            turned[k * units : (k + 1) * units, :], block, preferred_element_type=F32
        )


def weight_grads(rows, normed, cotangent, behind):
    units, width = rows[0].shape[1], normed[0].shape[1]
    block = min(width, 512)
    whole = lambda a: pl.BlockSpec(a.shape, lambda i: (0, 0))
    columns = lambda a: pl.BlockSpec((a.shape[0], block), lambda i: (0, i))
    return pl.pallas_call(
        grad_kernel,
        grid=(width // block,),
        in_specs=[whole(a) for a in rows]
        + [columns(a) for a in (*normed, *cotangent)]
        + [pl.BlockSpec(memory_space=pl.ANY)] * len(behind),
        out_specs=[pl.BlockSpec((units, block), lambda i: (0, i))] * 3
        + [pl.BlockSpec((8, width), lambda i: (0, 0))],
        out_shape=[jax.ShapeDtypeStruct((units, width), F32)] * 3
        + [jax.ShapeDtypeStruct((8, width), F32)],
        scratch_shapes=[pltpu.VMEM((3 * units, 2 * rows[0].shape[0]), BF16)],
        compiler_params=pltpu.CompilerParams(vmem_limit_bytes=24 * 2**20),
        cost_estimate=pl.CostEstimate(flops=1, bytes_accessed=60_000_000, transcendentals=0),
        name="weight_grads",
    )(*rows, *normed, *cotangent, *behind)


def add_kernel(kept_ref, got_ref, *refs):
    refs[-1][...] = kept_ref[...] + got_ref[...].astype(F32)


def add_got(kept, got, bytes_accessed, behind=()):
    return pl.pallas_call(
        add_kernel,
        in_specs=[pl.BlockSpec(memory_space=pltpu.VMEM)] * 2
        + [pl.BlockSpec(memory_space=pl.ANY)] * len(behind),
        out_shape=jax.ShapeDtypeStruct(kept.shape, F32),
        compiler_params=pltpu.CompilerParams(vmem_limit_bytes=8 * 2**20),
        cost_estimate=pl.CostEstimate(flops=1, bytes_accessed=bytes_accessed, transcendentals=0),
        name="add_got",
    )(kept, got, *behind)


def gain_kernel(*refs):
    products, inputs, gain, out = refs[:3], refs[3:5], refs[5], refs[6]
    half = products[0].shape[0]
    rows = [inputs[0][:half], inputs[0][half:], inputs[1][...]]
    total = jnp.zeros(out.shape, F32)
    for product, tokens in zip(products, rows):
        terms = product[...].astype(F32) * tokens.astype(F32)
        total = total + jnp.sum(terms, axis=0, keepdims=True)
    out[...] = total / gain[...]


def gain_sums(products, inputs, gain):
    out = pl.pallas_call(
        gain_kernel,
        out_shape=jax.ShapeDtypeStruct((1, gain.shape[0]), F32),
        compiler_params=pltpu.CompilerParams(vmem_limit_bytes=8 * 2**20),
        cost_estimate=pl.CostEstimate(flops=1000, bytes_accessed=1000, transcendentals=0),
        name="gain_sums",
    )(*products, *inputs, gain[None, :])
    return out


def after(value, dep):
    width = value.shape[1]
    if dep.shape[1] >= width:
        row = lax.slice(dep, (0, 0), (1, width))
    else:
        row = lax.slice(dep, (0, 0), (1, math.gcd(dep.shape[1], width)))
        row = jnp.tile(row, (1, width // row.shape[1]))
    return jnp.where(row == row, value, jnp.zeros_like(value))


def on_device(dp, node, tokens, cotangent, norm_gain, gate_weight, up_weight, down_weight):
    features = tokens.shape[1] * node
    widened = tokens.astype(F32)
    square_sum = jnp.sum(widened * widened, axis=1)
    bit = 1
    while bit < node:
        square_sum = square_sum + swap(square_sum, "node", node, bit)
        bit *= 2
    inv_rms = lax.rsqrt(square_sum / features + EPSILON)[:, None]
    scaled = widened * inv_rms
    normed_rows = (scaled * norm_gain).astype(BF16)
    own_n = gather_rows(normed_rows, dp)
    size = own_n.shape[0] // 2
    other_n = swap(own_n, "dp", dp, 1)

    def project(rows):
        return jnp.concatenate([inward(rows, gate_weight), inward(rows, up_weight)], axis=0)

    own_p = project(own_n)
    other_p = project(other_n)
    own_c = gather_rows_behind(cotangent, dp, own_p[2 * size :])
    other_c = swap(own_c, "dp", dp, 1)
    other_b = after(inward(other_c, down_weight), other_p)
    own_b = after(inward(own_c, down_weight), other_b)
    own_p = after(node_sum(own_p, node), own_b)
    other_p, own_b = node_sum(other_p, node), node_sum(own_b, node)

    def activate(both):
        gate_value, up_value = both[: 2 * size], both[2 * size :]
        activated, slope = gelu_parts(gate_value)
        hidden = (activated * up_value).astype(BF16)
        lean = slope * up_value
        row_factor = lean * gate_value + activated * up_value
        return lax.optimization_barrier((hidden, activated, lean, row_factor))

    def grads(back, activated, lean, row_factor):
        grad_gate, grad_up = (back * lean).astype(BF16), (back * activated).astype(BF16)
        row_part = jnp.sum(back * row_factor, axis=1)[None, :]
        return lax.optimization_barrier(((grad_gate, grad_up), row_part))

    def outward_pair(pair):
        return outward(pair[0], gate_weight) + outward(pair[1], up_weight)

    own_h, *own_f = activate(own_p)
    other_h, *other_f = activate(other_p)
    sent_h = outward(other_h, down_weight).astype(BF16)
    got_h = swap(sent_h, "dp", dp, 1)
    own_kept, own_sent = halve(own_h)
    got_kept, got_sent = halve(got_h)
    branch_sent = outward(own_sent, down_weight) + got_sent.astype(F32)
    branch_sent = lax.optimization_barrier(branch_sent.astype(BF16))
    branch = outward(own_kept, down_weight) + got_kept.astype(F32)
    bit = 1
    while bit < node:
        got = swap(other_b.astype(BF16), "node", node, bit)
        other_b = add_got(other_b, got, 40_000_000, (sent_h,))
        bit *= 2
    other_g, other_r = grads(other_b, *other_f)
    sent_g = outward_pair(other_g).astype(BF16)
    got_g = swap(sent_g, "dp", dp, 1)
    own_b = after(after(own_b, branch_sent), sent_g)
    own_g, own_r = grads(own_b, *own_f)
    normed_y = outward_pair([rows[size:] for rows in own_g])
    normed_sent = lax.optimization_barrier((normed_y + got_g[size:].astype(F32)).astype(BF16))
    normed_own = outward_pair([after(rows[:size], normed_sent) for rows in own_g])
    gain_part = gain_sums((normed_own, normed_y, sent_g), (own_n, other_n), norm_gain)
    width = gain_part.shape[1]

    def vector(distance, gain, rows):
        return swap(jnp.concatenate([gain, rows], axis=1), "dp", dp, distance)

    got_v = [
        vector(1, gain_part, other_r[:, :size]),
        vector(2, gain_part, own_r[:, size:]),
        vector(3, gain_part, other_r[:, size:]),
    ]
    first, *others = halving_distances(dp)
    branch = add_got(branch, swap(branch_sent, "dp", dp, first), 40_000_000, (gain_part,))
    for distance in (2, *others[:-1]):
        half = branch.shape[0] // 2
        sent_h = lax.optimization_barrier(branch[half:].astype(BF16))
        branch = branch[:half] + swap(sent_h, "dp", dp, distance).astype(F32)

    normed = normed_own + got_g[:size].astype(F32)
    normed = add_got(normed, swap(normed_sent, "dp", dp, 2), 40_000_000)
    normed = after(normed, sent_h)
    vectors = jnp.concatenate([after(gain_part, normed), own_r[:, :size]], axis=1)
    vectors = vectors + (got_v[0] + got_v[1] + got_v[2])
    gain_part, rows = vectors[:, :width], vectors[:, width:]
    for parts in direct_steps(dp):
        count = normed.shape[0] // (len(parts) + 1)
        extra = gain_part.reshape(count, -1)
        lanes = extra.shape[1]

        def joined(place):
            own_rows = rows[:, place * count : (place + 1) * count]
            return [
                normed[place * count : (place + 1) * count],
                extra,
                jnp.pad(own_rows, ((0, count - 1), (0, 0))),
            ]

        sent = [jnp.concatenate(joined(k + 1), axis=1).astype(BF16) for k in range(len(parts))]
        if count == tokens.shape[0]:
            for distance in others[-1:]:
                sent_h = after(branch[count:].astype(BF16), sent[0])
                branch = branch[:count] + swap(sent_h, "dp", dp, distance).astype(F32)
            grad_gate_weight, grad_up_weight, grad_down_weight, sent_h = weight_grads(
                (*own_g, own_h, *other_g, other_h),
                (own_n, other_n),
                (own_c, other_c),
                (sent[-1], sent_h),
            )
        kept, *extras = joined(0)
        total = jnp.concatenate([after(kept, sent_h), *extras], axis=1)
        for part, distance in zip(sent, parts):
            total = total + swap(part, "dp", dp, distance).astype(F32)
        normed = total[:, :width]
        gain_part = total[:, width : width + lanes].reshape(1, width)
        rows = total[:1, width + lanes :]

    row_mean = (rows / features).reshape(-1, 1)
    grad_scaled = normed * norm_gain
    grad_tokens = (inv_rms * (grad_scaled - scaled * row_mean)).astype(BF16)
    return (
        branch.astype(BF16),
        grad_tokens,
        grad_gate_weight,
        grad_up_weight,
        grad_down_weight,
        gain_part[0],
    )


def solution(mesh):
    dp, node = mesh.shape["dp"], mesh.shape["node"]

    def run(*arrays):
        return on_device(dp, node, *arrays)

    grid = P("dp", "node")
    return jax.shard_map(
        run,
        mesh=mesh,
        in_specs=(grid, grid, P("node"), grid, grid, grid),
        out_specs=(grid, grid, grid, grid, grid, P("node")),
        check_vma=False,
    )
```

```python
import functools
import math

import jax
import jax.numpy as jnp
from jax import lax
from jax.experimental import pallas as pl
from jax.experimental.pallas import tpu as pltpu
from jax.sharding import PartitionSpec as P

EPSILON = 1e-06
GELU_SCALE = math.sqrt(2.0 / math.pi)
BF16 = jnp.bfloat16
F32 = jnp.float32


def gelu_parts(value):
    inner = GELU_SCALE * (value + 0.044715 * value * value * value)
    tanh_inner = jnp.tanh(inner)
    activated = 0.5 * value * (1.0 + tanh_inner)
    slope = 0.5 * (1.0 + tanh_inner) + 0.5 * value * (
        1.0 - tanh_inner * tanh_inner
    ) * GELU_SCALE * (1.0 + 3.0 * 0.044715 * value * value)
    return (activated, slope)


def swap(value, axis, size, distance):
    return lax.ppermute(value, axis, [(i, i ^ distance) for i in range(size)])


def node_sum(value, node):
    bit = 1
    while bit < node:
        value = value + swap(value.astype(BF16), "node", node, bit).astype(F32)
        bit *= 2
    return value


def halving_distances(dp):
    distances = []
    bit = 4
    while bit < dp:
        distances.append(bit)
        bit *= 2
    return distances


def direct_steps(dp):
    distances, steps = halving_distances(dp), []
    while distances:
        low, *high = distances[:2]
        steps.append([high[0], low, low ^ high[0]] if high else [low])
        distances = distances[2:]
    return steps


def halve(rows):
    half, quarter = rows.shape[0] // 2, rows.shape[0] // 4
    kept = jnp.concatenate([rows[:quarter], rows[half : half + quarter]], axis=0)
    return kept, jnp.concatenate([rows[quarter:half], rows[half + quarter :]], axis=0)


def gather_rows(rows, dp):
    for parts in reversed(direct_steps(dp)):
        rows = jnp.concatenate([rows] + [swap(rows, "dp", dp, d) for d in parts], axis=0)
    return jnp.concatenate([rows, swap(rows, "dp", dp, 2)], axis=0)


def gather_rows_behind(rows, dp, used_behind):
    for distance in reversed(halving_distances(dp)):
        rows = jnp.concatenate([rows, swap(rows, "dp", dp, distance)], axis=0)
    got = swap(rows, "dp", dp, 2)
    return jnp.concatenate([rows, after(got, used_behind)], axis=0)


def inward(rows, weight):
    return lax.dot_general(rows, weight, (((1,), (1,)), ((), ())), preferred_element_type=F32)


def outward(rows, weight):
    return lax.dot_general(rows, weight, (((1,), (0,)), ((), ())), preferred_element_type=F32)


def grad_kernel(*refs):
    rows, normed, cotangent = refs[:6], refs[6:8], refs[8:10]
    outs, (mark, turned) = refs[-5:-2], refs[-2:]
    half, units = rows[0].shape

    @pl.when(jnp.logical_and(pl.program_id(0) == 0, pl.program_id(1) == 0))
    def _():
        mark[...] = jnp.zeros(mark.shape, F32)

    for k, inputs in enumerate((normed, normed, cotangent)):

        @pl.when(pl.program_id(0) == k)
        def _():
            @pl.when(pl.program_id(1) == 0)
            def _():
                turned[:, :half] = rows[k][...].T
                turned[:, half:] = rows[3 + k][...].T

            block = jnp.concatenate([ref[...] for ref in inputs], axis=0)
            outs[k][...] = jnp.dot(turned[...], block, preferred_element_type=F32)


def weight_grads(rows, normed, cotangent, behind):
    units, width = rows[0].shape[1], normed[0].shape[1]
    block = min(width, 512)
    steps = width // block
    whole = lambda a: pl.BlockSpec(a.shape, lambda k, i: (0, 0))

    def columns(height, first, last):
        def place(k, i):
            return (0, jnp.where(k < first, 0, jnp.where(k > last, steps - 1, i)))

        return pl.BlockSpec((height, block), place)

    return pl.pallas_call(
        grad_kernel,
        grid=(3, steps),
        in_specs=[whole(a) for a in rows]
        + [columns(a.shape[0], 0, 1) for a in normed]
        + [columns(a.shape[0], 2, 2) for a in cotangent]
        + [pl.BlockSpec(memory_space=pl.ANY)] * len(behind),
        out_specs=[columns(units, k, k) for k in range(3)]
        + [pl.BlockSpec((8, width), lambda k, i: (0, 0))],
        out_shape=[jax.ShapeDtypeStruct((units, width), F32)] * 3
        + [jax.ShapeDtypeStruct((8, width), F32)],
        scratch_shapes=[pltpu.VMEM((units, 2 * rows[0].shape[0]), BF16)],
        compiler_params=pltpu.CompilerParams(vmem_limit_bytes=24 * 2**20),
        cost_estimate=pl.CostEstimate(flops=1, bytes_accessed=60_000_000, transcendentals=0),
        name="weight_grads",
    )(*rows, *normed, *cotangent, *behind)


def add_kernel(kept_ref, got_ref, *refs):
    refs[-1][...] = kept_ref[...] + got_ref[...].astype(F32)


def add_got(kept, got, bytes_accessed, behind=()):
    return pl.pallas_call(
        add_kernel,
        in_specs=[pl.BlockSpec(memory_space=pltpu.VMEM)] * 2
        + [pl.BlockSpec(memory_space=pl.ANY)] * len(behind),
        out_shape=jax.ShapeDtypeStruct(kept.shape, F32),
        compiler_params=pltpu.CompilerParams(vmem_limit_bytes=8 * 2**20),
        cost_estimate=pl.CostEstimate(flops=1, bytes_accessed=bytes_accessed, transcendentals=0),
        name="add_got",
    )(kept, got, *behind)


def gain_kernel(*refs):
    products, inputs, gain, out = refs[:3], refs[3:5], refs[5], refs[6]
    half = products[0].shape[0]
    rows = [inputs[0][:half], inputs[0][half:], inputs[1][...]]
    total = jnp.zeros(out.shape, F32)
    for product, tokens in zip(products, rows):
        terms = product[...].astype(F32) * tokens.astype(F32)
        total = total + jnp.sum(terms, axis=0, keepdims=True)
    out[...] = total / gain[...]


def gain_sums(products, inputs, gain):
    out = pl.pallas_call(
        gain_kernel,
        out_shape=jax.ShapeDtypeStruct((1, gain.shape[0]), F32),
        compiler_params=pltpu.CompilerParams(vmem_limit_bytes=8 * 2**20),
        cost_estimate=pl.CostEstimate(flops=1000, bytes_accessed=1000, transcendentals=0),
        name="gain_sums",
    )(*products, *inputs, gain[None, :])
    return out


def after(value, dep):
    width = value.shape[1]
    if dep.shape[1] >= width:
        row = lax.slice(dep, (0, 0), (1, width))
    else:
        row = lax.slice(dep, (0, 0), (1, math.gcd(dep.shape[1], width)))
        row = jnp.tile(row, (1, width // row.shape[1]))
    return jnp.where(row == row, value, jnp.zeros_like(value))


def on_device(dp, node, tokens, cotangent, norm_gain, gate_weight, up_weight, down_weight):
    features = tokens.shape[1] * node
    widened = tokens.astype(F32)
    square_sum = jnp.sum(widened * widened, axis=1)
    bit = 1
    while bit < node:
        square_sum = square_sum + swap(square_sum, "node", node, bit)
        bit *= 2
    inv_rms = lax.rsqrt(square_sum / features + EPSILON)[:, None]
    scaled = widened * inv_rms
    normed_rows = (scaled * norm_gain).astype(BF16)
    own_n = gather_rows(normed_rows, dp)
    size = own_n.shape[0] // 2
    other_n = swap(own_n, "dp", dp, 1)

    def project(rows):
        return jnp.concatenate([inward(rows, gate_weight), inward(rows, up_weight)], axis=0)

    own_p = project(own_n)
    other_p = project(other_n)
    own_c = gather_rows_behind(cotangent, dp, own_p[2 * size :])
    other_c = swap(own_c, "dp", dp, 1)
    other_b = after(inward(other_c, down_weight), other_p)
    own_b = after(inward(own_c, down_weight), other_b)
    own_p = after(node_sum(own_p, node), own_b)
    other_p, own_b = node_sum(other_p, node), node_sum(own_b, node)

    def activate(both):
        gate_value, up_value = both[: 2 * size], both[2 * size :]
        activated, slope = gelu_parts(gate_value)
        hidden = (activated * up_value).astype(BF16)
        lean = slope * up_value
        row_factor = lean * gate_value + activated * up_value
        return lax.optimization_barrier((hidden, activated, lean, row_factor))

    def grads(back, activated, lean, row_factor):
        grad_gate, grad_up = (back * lean).astype(BF16), (back * activated).astype(BF16)
        row_part = jnp.sum(back * row_factor, axis=1)[None, :]
        return lax.optimization_barrier(((grad_gate, grad_up), row_part))

    def outward_pair(pair):
        return outward(pair[0], gate_weight) + outward(pair[1], up_weight)

    own_h, *own_f = activate(own_p)
    other_h, *other_f = activate(other_p)
    sent_h = outward(other_h, down_weight).astype(BF16)
    got_h = swap(sent_h, "dp", dp, 1)
    own_kept, own_sent = halve(own_h)
    got_kept, got_sent = halve(got_h)
    branch_sent = outward(own_sent, down_weight) + got_sent.astype(F32)
    branch_sent = lax.optimization_barrier(branch_sent.astype(BF16))
    branch = outward(own_kept, down_weight) + got_kept.astype(F32)
    bit = 1
    while bit < node:
        got = swap(other_b.astype(BF16), "node", node, bit)
        other_b = add_got(other_b, got, 40_000_000, (sent_h,))
        bit *= 2
    other_g, other_r = grads(other_b, *other_f)
    sent_g = outward_pair(other_g).astype(BF16)
    got_g = swap(sent_g, "dp", dp, 1)
    own_b = after(after(own_b, branch_sent), sent_g)
    own_g, own_r = grads(own_b, *own_f)
    normed_y = outward_pair([rows[size:] for rows in own_g])
    normed_sent = lax.optimization_barrier((normed_y + got_g[size:].astype(F32)).astype(BF16))
    normed_own = outward_pair([after(rows[:size], normed_sent) for rows in own_g])
    gain_part = gain_sums((normed_own, normed_y, sent_g), (own_n, other_n), norm_gain)
    width = gain_part.shape[1]

    def vector(distance, gain, rows):
        return swap(jnp.concatenate([gain, rows], axis=1), "dp", dp, distance)

    got_v = [
        vector(1, gain_part, other_r[:, :size]),
        vector(2, gain_part, own_r[:, size:]),
        vector(3, gain_part, other_r[:, size:]),
    ]
    first, *others = halving_distances(dp)
    branch = add_got(branch, swap(branch_sent, "dp", dp, first), 40_000_000, (gain_part,))
    for distance in (2, *others[:-1]):
        half = branch.shape[0] // 2
        sent_h = lax.optimization_barrier(branch[half:].astype(BF16))
        branch = branch[:half] + swap(sent_h, "dp", dp, distance).astype(F32)

    normed = normed_own + got_g[:size].astype(F32)
    normed = add_got(normed, swap(normed_sent, "dp", dp, 2), 40_000_000)
    normed = after(normed, sent_h)
    vectors = jnp.concatenate([after(gain_part, normed), own_r[:, :size]], axis=1)
    vectors = vectors + (got_v[0] + got_v[1] + got_v[2])
    gain_part, rows = vectors[:, :width], vectors[:, width:]
    for parts in direct_steps(dp):
        count = normed.shape[0] // (len(parts) + 1)
        extra = gain_part.reshape(count, -1)
        lanes = extra.shape[1]

        def joined(place):
            own_rows = rows[:, place * count : (place + 1) * count]
            return [
                normed[place * count : (place + 1) * count],
                extra,
                jnp.pad(own_rows, ((0, count - 1), (0, 0))),
            ]

        sent = [jnp.concatenate(joined(k + 1), axis=1).astype(BF16) for k in range(len(parts))]
        if count == tokens.shape[0]:
            for distance in others[-1:]:
                sent_h = after(branch[count:].astype(BF16), sent[0])
                branch = branch[:count] + swap(sent_h, "dp", dp, distance).astype(F32)
            grad_gate_weight, grad_up_weight, grad_down_weight, sent_h = weight_grads(
                (*own_g, own_h, *other_g, other_h),
                (own_n, other_n),
                (own_c, other_c),
                (sent[-1], sent_h),
            )
        kept, *extras = joined(0)
        total = jnp.concatenate([after(kept, sent_h), *extras], axis=1)
        for part, distance in zip(sent, parts):
            total = total + swap(part, "dp", dp, distance).astype(F32)
        normed = total[:, :width]
        gain_part = total[:, width : width + lanes].reshape(1, width)
        rows = total[:1, width + lanes :]

    row_mean = (rows / features).reshape(-1, 1)
    grad_scaled = normed * norm_gain
    grad_tokens = (inv_rms * (grad_scaled - scaled * row_mean)).astype(BF16)
    return (
        branch.astype(BF16),
        grad_tokens,
        grad_gate_weight,
        grad_up_weight,
        grad_down_weight,
        gain_part[0],
    )


def solution(mesh):
    dp, node = mesh.shape["dp"], mesh.shape["node"]

    def run(*arrays):
        return on_device(dp, node, *arrays)

    grid = P("dp", "node")
    return jax.shard_map(
        run,
        mesh=mesh,
        in_specs=(grid, grid, P("node"), grid, grid, grid),
        out_specs=(grid, grid, grid, grid, grid, P("node")),
        check_vma=False,
    )
```
